512 devices in a mesh: ctx: 64 (over z, y), head: 8 (over x, core).
Axes of the slice: x: 4, y: 4, z: 16, core: 2. Of those that a mesh axis runs over, the one named last changes fastest.
Arguments:
- queries: bfloat16 [16384, 4096], P('ctx', 'head'), may hold values from -6 to 6
- keys: bfloat16 [16384, 4096], P('ctx', 'head'), may hold values from -6 to 6
- values: bfloat16 [16384, 4096], P('ctx', 'head'), may hold values from -6 to 6
- out_grad: bfloat16 [16384, 4096], P('ctx', 'head'), may hold values from -6 to 6
- out_weight: bfloat16 [16, 256, 4096], P('head', 'ctx'), may hold values from -0.09375 to 0.09375
- decay_rate: float32 [16], P('head'), may hold values from 0.00024414062 to 0.025
- doc_spans: int32 [21], replicated, may hold values from 1 to 4, 64 in all
Outputs:
- query_grad: bfloat16 [16384, 4096], P('ctx', 'head')
- key_grad: bfloat16 [16384, 4096], P('ctx', 'head')
- value_grad: bfloat16 [16384, 4096], P('ctx', 'head')
The draws below stay inside these ranges and needn't reach their ends.
Inputs may be any that keep to these rules, and one draw needn't show every extreme that they name: `doc_spans`: each length counts whole spans of 256 tokens; the lengths sum to 64 and the longest is exactly 4.
All inputs are finite; a program needn't handle non-finite values.
Results may differ from the reference program's by a relative error of at most 0.007.
Values may be sent and summed in bfloat16 or wider, within the bound.
No kernel may reach another device: no remote copies, remote signals or barrier semaphores. Data moves between devices by JAX's collectives and lax.ppermute only.
A program may use at most 128 MiB of HBM per device.

```python
import math
import jax
import jax.numpy as jnp
import numpy as np
from jax import lax

D = 4096
H = 16
DK = 256
DV = 256
SPAN = 256
SPANS = 64
TOKENS = 16384
MAXDOC = 4
NDOC = 21


def steps_of(stream_key, extent, cuts, low, high):
    gain = 1.0
    for dim, blocks in cuts:
        steps = jax.random.uniform(jax.random.fold_in(jax.random.fold_in(stream_key, 6), dim), (blocks,), jnp.float32, low / len(cuts), high / len(cuts))
        gain = gain * jnp.repeat(jnp.exp(steps), extent[dim] // blocks).reshape((-1,) + (1,) * (len(extent) - 1 - dim))
    return gain


def profile(amount, total, limit, slope):
    weights = [(1 << 20) // math.isqrt(standing ** slope) + 1 for standing in range(2, amount + 1)]
    rest, counts = total - limit - (amount - 1), [1] * (amount - 1)
    while rest > 0:
        candidates = [i for i in range(amount - 1) if counts[i] < limit]
        mass, remaining = sum([weights[i] for i in candidates]), rest
        for i in candidates:
            more = min(limit - counts[i], max(1, remaining * weights[i] // mass), rest)
            counts[i] = counts[i] + more
            rest = rest - more
    return np.array([limit] + counts)


def uneven(own_key, count, total, bound, slope):
    if count == 2:
        one = jax.random.randint(own_key, (), max(1, total - bound), min(bound, total - 1) + 1)
        return jnp.stack([one, total - one])
    lengths = jnp.asarray(profile(count, total, bound, slope), jnp.int32)
    pairs = (count - 1) // 2
    source_of, sink = lengths[1:1 + 2 * pairs:2], lengths[2:2 + 2 * pairs:2]
    room = jnp.minimum(source_of - 1, bound - sink)
    passed = jax.random.randint(jax.random.fold_in(own_key, 1), (pairs,), 0, 1 << 20) % (room + 1)
    lengths = lengths.at[1:1 + 2 * pairs:2].set(source_of - passed).at[2:2 + 2 * pairs:2].set(sink + passed)
    return lengths[jax.random.permutation(jax.random.fold_in(own_key, 2), count)]


def bell_draw(own_key, dims, scale, reach, shards=(), kind=jnp.bfloat16):
    entries = scale * jax.random.normal(own_key, dims, jnp.float32)
    if shards:
        entries = entries * steps_of(own_key, dims, shards, -0.22, 0.18)
    return jnp.clip(entries, -reach, reach).astype(kind)


def setup_inputs(seed: int = 0) -> dict:
    key_of = jax.random.split(jax.random.key(seed), 8)
    queries = bell_draw(key_of[0], (TOKENS, H * DK), 1.0, 6.0, ((0, 64), (1, 8)))
    keys = bell_draw(key_of[1], (TOKENS, H * DK), 1.0, 6.0, ((0, 64), (1, 8)))
    values = bell_draw(key_of[2], (TOKENS, H * DV), 1.0, 6.0, ((0, 64), (1, 8)))
    out_grad = bell_draw(key_of[3], (TOKENS, D), 1.0, 6.0, ((0, 64), (1, 8)))
    out_weight = bell_draw(key_of[4], (H, DV, D), D ** -0.5, 0.09375, ((0, 8), (1, 64)))
    decay_rate = jnp.clip(jnp.exp(math.log(0.025) - 4.6288867 * jax.random.uniform(key_of[5], (H,), jnp.float32) ** steps_of(key_of[5], (H,), ((0, 8),), -0.2, 0.2)), 0.00024414062, 0.025)
    doc_spans = uneven(key_of[6], NDOC, SPANS, MAXDOC, 0).astype(jnp.int32)
    return {"queries": queries, "keys": keys, "values": values, "out_grad": out_grad, "out_weight": out_weight, "decay_rate": decay_rate, "doc_spans": doc_spans}


EPS = 1e-05
PREC = lax.Precision.HIGHEST

def decay_tables(decay_rate):
    offset = jnp.arange(SPAN, dtype=jnp.float32)
    distance = offset[:, None] - offset[None, :]
    decay_mask = jnp.where(distance[None] >= 0.0, jnp.exp(-decay_rate[:, None, None] * jnp.maximum(distance, 0.0)[None]), 0.0)
    query_decay = jnp.exp(-decay_rate[:, None] * offset[None, :]).T
    key_decay = jnp.exp(-decay_rate[:, None] * (SPAN - offset)[None, :]).T
    whole_decay = jnp.exp(-decay_rate * SPAN)
    return (decay_mask, query_decay, key_decay, whole_decay)

def span_starts(doc_spans, total):
    firsts = (jnp.cumsum(doc_spans) - doc_spans).astype(jnp.int32)
    return jnp.any(jnp.arange(total, dtype=jnp.int32)[:, None] == firsts[None, :], axis=1)

def group_norm(output):
    centred = output - lax.optimization_barrier(jnp.mean(output, axis=-1, keepdims=True))
    variance = lax.optimization_barrier(jnp.mean(centred * centred, axis=-1, keepdims=True))
    return centred * lax.rsqrt(variance + EPS)

def reference(queries, keys, values, out_grad, out_weight, decay_rate, doc_spans):
    scale = DK ** (-0.5)
    decay_mask, query_decay, key_decay, whole_decay = decay_tables(decay_rate)
    starts = span_starts(doc_spans, SPANS)
    next_starts = jnp.concatenate([starts[1:], jnp.ones((1,), dtype=bool)])
    q_all = queries.astype(jnp.float32).reshape(SPANS, SPAN, H, DK)
    k_all = keys.astype(jnp.float32).reshape(SPANS, SPAN, H, DK)
    v_all = values.astype(jnp.float32).reshape(SPANS, SPAN, H, DV)

    def make_weights(q_block, k_block):
        raw = jnp.einsum('thd,shd->hts', q_block, k_block, precision=PREC)
        return (raw * scale * decay_mask).astype(jnp.bfloat16).astype(jnp.float32)

    def forward(state, inputs):
        q_block, k_block, v_block, begins = inputs
        state = jnp.where(begins, 0.0, state)
        weights = make_weights(q_block, k_block)
        output = jnp.einsum('hts,she->the', weights, v_block, precision=PREC)
        output = output + scale * query_decay[:, :, None] * jnp.einsum('thd,hde->the', q_block, state, precision=PREC)
        update = jnp.einsum('shd,she->hde', k_block * key_decay[:, :, None], v_block, precision=PREC)
        return (whole_decay[:, None, None] * state + update, (output, state))
    zero_state = jnp.zeros((H, DK, DV), jnp.float32)
    _, (retained, states_in) = lax.scan(forward, zero_state, (q_all, k_all, v_all, starts))
    flat_weight = out_weight.reshape(H * DV, D)
    norm_grad = jnp.dot(out_grad, flat_weight.T, preferred_element_type=jnp.float32).reshape(SPANS, SPAN, H, DV)
    _, pullback = jax.vjp(group_norm, retained)
    retained_grad = pullback(norm_grad)[0]

    def backward(later, inputs):
        q_block, k_block, v_block, g_block, state, ends_here = inputs
        incoming = jnp.where(ends_here, 0.0, later)
        g_round = lax.optimization_barrier(g_block.astype(jnp.bfloat16)).astype(jnp.float32)
        raw_grad = jnp.einsum('the,she->hts', g_round, v_block, precision=PREC) * decay_mask
        dscores = lax.optimization_barrier(raw_grad.astype(jnp.bfloat16)).astype(jnp.float32)
        weights = make_weights(q_block, k_block)
        q_grad = jnp.einsum('hts,shd->thd', dscores, k_block, precision=PREC)
        q_grad = q_grad + query_decay[:, :, None] * jnp.einsum('hde,the->thd', state, g_block, precision=PREC)
        k_grad = jnp.einsum('hts,thd->shd', dscores, q_block, precision=PREC)
        k_grad = k_grad + key_decay[:, :, None] * jnp.einsum('hde,she->shd', incoming, v_block, precision=PREC)
        v_grad = jnp.einsum('hts,the->she', weights, g_round, precision=PREC)
        v_grad = v_grad + scale * key_decay[:, :, None] * jnp.einsum('hde,shd->she', incoming, k_block, precision=PREC)
        source = jnp.einsum('thd,the->hde', q_block * query_decay[:, :, None], g_block, precision=PREC)
        total = whole_decay[:, None, None] * incoming + source
        return (total, (scale * q_grad, scale * k_grad, v_grad))
    _, (q_grads, k_grads, v_grads) = lax.scan(backward, zero_state, (q_all, k_all, v_all, retained_grad, states_in, next_starts), reverse=True)
    query_grad = q_grads.reshape(TOKENS, H * DK).astype(jnp.bfloat16)
    key_grad = k_grads.reshape(TOKENS, H * DK).astype(jnp.bfloat16)
    value_grad = v_grads.reshape(TOKENS, H * DV).astype(jnp.bfloat16)
    return (query_grad, key_grad, value_grad)
```

```python
import jax
import jax.numpy as jnp
from jax import lax
from jax.experimental import pallas as pl
from jax.experimental.pallas import tpu as pltpu
from jax.sharding import Mesh, PartitionSpec as P

DK = 256
DV = 256
SPAN = 256
HEADS = 2
REACH = 3
EPS = 1e-05
SCALE = DK**-0.5
F32 = jnp.float32
BF16 = jnp.bfloat16
PREC = lax.Precision.HIGHEST
NEAR = (0, 1, -1, 2)
LOW = 32
SENT = SPAN + LOW

Z1, Z0, Y, X, CORE = 4, 4, 4, 4, 2
Z = Z1 * Z0
DEPTH = ("z1", "z0")
CTX = ("z1", "z0", "y")
HEAD = ("x", "core")

SMEM = pl.BlockSpec(memory_space=pltpu.SMEM)
VMEM = pl.BlockSpec(memory_space=pltpu.VMEM)
HBM = pl.BlockSpec(memory_space=pltpu.HBM)
ANY = pl.BlockSpec(memory_space=pl.ANY)


def dot(a, b, dims, precision=None):
    return lax.dot_general(a, b, ((dims[:1], dims[1:]), ((), ())), precision=precision, preferred_element_type=F32)


def nn(a, b, precision=None):
    return dot(a, b, (1, 0), precision)


def nt(a, b, precision=None):
    return dot(a, b, (1, 1), precision)


def tn(a, b, precision=None):
    return dot(a, b, (0, 0), precision)


def cols(h):
    return slice(h * 256, (h + 1) * 256)


def offsets():
    return lax.broadcasted_iota(jnp.int32, (SPAN, 1), 0).astype(F32)


def decay_mask(rate):
    t = lax.broadcasted_iota(jnp.int32, (SPAN, SPAN), 0)
    s = lax.broadcasted_iota(jnp.int32, (SPAN, SPAN), 1)
    distance = jnp.maximum(t - s, 0).astype(F32)
    return jnp.where(t >= s, jnp.exp(-rate * distance), 0.0)


def joined(spans_ref, towards):
    place = (lax.axis_index("z1") * Z0 + lax.axis_index("z0")) * Y + lax.axis_index("y")
    edges = [place + 1 + j if towards > 0 else place - j for j in range(REACH)]
    cut = [jnp.int32(0)] * REACH
    first = jnp.int32(0)
    for i in range(spans_ref.shape[0] + 1):
        cut = [c + (first == e).astype(jnp.int32) for c, e in zip(cut, edges)]
        if i < spans_ref.shape[0]:
            first = first + spans_ref[i]
    out, total = [], jnp.int32(0)
    for c in cut:
        total = total + c
        out.append(jnp.where(total == 0, 1.0, 0.0).astype(F32))
    return out


def combined(states, links, rate, h):
    total = links[0] * states[0][:, cols(h)].astype(F32)
    for j in range(1, REACH):
        fade = jnp.exp(jnp.full((1, DV), -rate * (SPAN * j), F32)) * links[j]
        total = total + fade * states[j][:, cols(h)].astype(F32)
    return total


def one_hot(target):
    return jnp.where(lax.broadcasted_iota(jnp.int32, (512, 512), 1) == target, 1.0, 0.0).astype(BF16)


def update_kernel(rate_ref, k_ref, v_ref, u_ref, sel_ref, order_ref):
    for h in range(HEADS):
        fade = jnp.exp(-rate_ref[h] * (SPAN - offsets()))
        k = k_ref[:, cols(h)].astype(F32) * fade
        u_ref[:, cols(h)] = tn(k, v_ref[:, cols(h)].astype(F32), PREC).astype(BF16)
    row = lax.broadcasted_iota(jnp.int32, (512, 1), 0)
    near = row // 128
    shift = jnp.where(near == 1, NEAR[1], jnp.where(near == 2, NEAR[2], jnp.where(near == 3, NEAR[3], NEAR[0])))
    z = (row // 32) % 4 * Z0 + (lax.axis_index("z0") + shift + Z0) % Z0
    sel_ref[...] = one_hot((row // 8) % 4 * 128 + (row // 4) % 2 * 64 + z * 4 + row % 4)
    order_ref[...] = one_hot((row // 64) % 2 * 256 + (row // 4) % 16 * 16 + row // 128 * 4 + row % 4)


def forward_kernel(rate_ref, spans_ref, q_ref, k_ref, v_ref, u1, u2, u3, normed_ref, rstd_ref, weights_ref, state_ref):
    links = joined(spans_ref, -1)
    for h in range(HEADS):
        rate = rate_ref[h]
        q, k, v = q_ref[:, cols(h)], k_ref[:, cols(h)], v_ref[:, cols(h)]
        weights = (nt(q, k) * SCALE * decay_mask(rate)).astype(BF16)
        weights_ref[:, cols(h)] = weights
        state = combined((u1, u2, u3), links, rate, h)
        state_ref[:, cols(h)] = state.astype(BF16)
        fade = SCALE * jnp.exp(-rate * offsets())
        out = nn(weights, v) + fade * nn(q.astype(F32), state, PREC)
        centred = out - jnp.mean(out, axis=1, keepdims=True)
        rstd = lax.rsqrt(jnp.mean(centred * centred, axis=1, keepdims=True) + EPS)
        normed_ref[:, cols(h)] = centred * rstd
        rstd_ref[:, h * 128 : (h + 1) * 128] = jnp.broadcast_to(rstd, (SPAN, 128))


def project_kernel(feat_ref, w0, w1, w2, w3, sel_ref, after_ref, out_ref, feat, sems):
    copies = []
    for y in range(Y):
        part = pl.ds(y * CORE, CORE)
        copies.append(pltpu.make_async_copy(feat_ref.at[part], feat.at[part], sems.at[y]))
        copies[y].start()
    rows = jnp.concatenate([w0[...], w1[...], w2[...], w3[...]], axis=0)
    weight = tn(rows, sel_ref[...]).astype(BF16)
    for y in range(Y):
        copies[y].wait()
        out = nn(feat[y * CORE], weight[:512, :]) + nn(feat[y * CORE + 1], weight[512:, :])
        high = out.astype(BF16)
        low = (out[:LOW] - high[:LOW].astype(F32)).astype(BF16)
        for x in range(X):
            out_ref[y * X + x, :SPAN] = high[:, x * 128 : (x + 1) * 128]
            out_ref[y * X + x, SPAN:] = low[:, x * 128 : (x + 1) * 128]


def norm_kernel(rate_ref, parts_ref, order_ref, normed_ref, rstd_ref, q_ref, g_ref, source_ref):
    sums = []
    for y in range(Y):
        total = parts_ref[y * X].astype(F32)
        for x in range(1, X):
            total = total + parts_ref[y * X + x].astype(F32)
        sums.append(jnp.concatenate([total[:LOW] + total[SPAN:], total[LOW:SPAN]], axis=0))
    whole = jnp.concatenate(sums, axis=1)
    high = whole.astype(BF16)
    low = (whole - high.astype(F32)).astype(BF16)
    norm_grad = nn(high, order_ref[...]) + nn(low, order_ref[...])
    for h in range(HEADS):
        grad = norm_grad[:, cols(h)]
        normed = normed_ref[:, cols(h)]
        rstd = rstd_ref[:, h * 128 : h * 128 + 1]
        inner = jnp.mean(normed * grad, axis=1, keepdims=True)
        g = rstd * (grad - jnp.mean(grad, axis=1, keepdims=True) - normed * inner)
        g_ref[:, cols(h)] = g.astype(BF16)
        fade = jnp.exp(-rate_ref[h] * offsets())
        source_ref[:, cols(h)] = tn(q_ref[:, cols(h)], (g * fade).astype(BF16)).astype(BF16)


def local_kernel(rate_ref, q_ref, k_ref, v_ref, g_ref, weights_ref, state_ref, qg_ref, kg_ref, vg_ref):
    for h in range(HEADS):
        rate = rate_ref[h]
        q, k, v, g = q_ref[:, cols(h)], k_ref[:, cols(h)], v_ref[:, cols(h)], g_ref[:, cols(h)]
        score = (nt(g, v) * decay_mask(rate)).astype(BF16)
        fade = jnp.exp(-rate * offsets())
        qg = nn(score, k) + fade * nt(g, state_ref[:, cols(h)])
        qg_ref[:, cols(h)] = (SCALE * qg).astype(BF16)
        kg_ref[:, cols(h)] = tn(score, q)
        vg_ref[:, cols(h)] = tn(weights_ref[:, cols(h)], g)


def final_kernel(rate_ref, spans_ref, s1, s2, s3, k_ref, v_ref, kg_ref, vg_ref, k_out, v_out):
    links = joined(spans_ref, 1)
    for h in range(HEADS):
        rate = rate_ref[h]
        later = combined((s1, s2, s3), links, rate, h).astype(BF16)
        fade = SCALE * jnp.exp(-rate * (SPAN - offsets()))
        k_out[:, cols(h)] = (SCALE * kg_ref[:, cols(h)] + fade * nt(v_ref[:, cols(h)], later)).astype(BF16)
        v_out[:, cols(h)] = (vg_ref[:, cols(h)] + fade * nn(k_ref[:, cols(h)], later)).astype(BF16)


def call(kernel, name, in_specs, outs, flops=0, room=32, **more):
    params = pltpu.CompilerParams(vmem_limit_bytes=room * 1024 * 1024)
    return pl.pallas_call(
        kernel,
        name=name,
        in_specs=in_specs,
        out_shape=outs,
        compiler_params=params,
        cost_estimate=pl.CostEstimate(flops=flops, bytes_accessed=2 << 20, transcendentals=0),
        **more,
    )


def sds(shape, dtype):
    return jax.ShapeDtypeStruct(shape, dtype)


def shift(x, axes, size, by):
    return lax.ppermute(x, axes, [(i, (i + by) % size) for i in range(size)])


def shards(queries, keys, values, out_grad, out_weight, decay_rate, doc_spans):
    block = (SPAN, HEADS * 256)
    split = jnp.broadcast_to(out_weight.reshape(8, X, 1024).transpose(1, 0, 2), (Z1, X, 8, 1024)).reshape(Z1 * X, 8, 1024)
    held = lax.all_to_all(split, ("z1", "x"), 0, 0).reshape(128, 1024)
    rows = [held] + [shift(held, DEPTH, Z, -s) for s in NEAR[1:]]
    features = lax.all_gather(out_grad, ("y", "core"), axis=0)

    update, sel, order = call(
        update_kernel,
        "update",
        [SMEM, VMEM, VMEM],
        [sds(block, BF16), sds((512, 512), BF16), sds((512, 512), BF16)],
        flops=1 << 28,
    )(decay_rate, keys, values)
    before = [shift(update, CTX, Z * Y, j) for j in range(1, REACH + 1)]
    normed, rstd, weights, state = call(
        forward_kernel,
        "forward",
        [SMEM, SMEM] + [VMEM] * 6,
        [sds(block, F32), sds((SPAN, 256), F32), sds(block, BF16), sds(block, BF16)],
        flops=1 << 29,
    )(decay_rate, doc_spans, queries, keys, values, *before)

    partial = call(
        project_kernel,
        "project",
        [HBM] + [VMEM] * 5 + [ANY],
        sds((Y * X, SENT, 128), BF16),
        flops=1 << 30,
        room=32,
        scratch_shapes=[pltpu.VMEM((Y * CORE, SPAN, 512), BF16), pltpu.SemaphoreType.DMA((Y,))],
    )(features, *rows, sel, state)
    parts = lax.all_to_all(partial, ("y", "x"), 0, 0)

    g, source = call(norm_kernel, "norm", [SMEM] + [VMEM] * 5, [sds(block, BF16)] * 2, flops=1 << 26)(
        decay_rate, parts, order, normed, rstd, queries
    )
    after = [shift(source, CTX, Z * Y, -j) for j in range(1, REACH + 1)]
    query_grad, kg, vg = call(
        local_kernel, "local", [SMEM] + [VMEM] * 6, [sds(block, BF16), sds(block, F32), sds(block, F32)], flops=1 << 28
    )(decay_rate, queries, keys, values, g, weights, state)
    key_grad, value_grad = call(final_kernel, "final", [SMEM, SMEM] + [VMEM] * 7, [sds(block, BF16)] * 2, flops=1 << 27)(
        decay_rate, doc_spans, *after, keys, values, kg, vg
    )
    return query_grad, key_grad, value_grad


def solution(mesh):
    fine = Mesh(mesh.devices.reshape(Z1, Z0, Y, X, CORE), ("z1", "z0", "y", "x", "core"))
    in_specs = (P(CTX, HEAD), P(CTX, HEAD), P(CTX, HEAD), P(CTX, HEAD), P(HEAD, CTX, None), P(HEAD), P())
    out_specs = (P(CTX, HEAD), P(CTX, HEAD), P(CTX, HEAD))
    return jax.shard_map(shards, mesh=fine, in_specs=in_specs, out_specs=out_specs, check_vma=False)
```

```python
import jax
import jax.numpy as jnp
from jax import lax
from jax.experimental import pallas as pl
from jax.experimental.pallas import tpu as pltpu
from jax.sharding import Mesh, PartitionSpec as P

DK = 256
DV = 256
SPAN = 256
HEADS = 2
REACH = 3
EPS = 1e-05
SCALE = DK**-0.5
F32 = jnp.float32
BF16 = jnp.bfloat16
PREC = lax.Precision.HIGHEST
NEAR = (0, 1, -1, 2)
LOW = 32
SENT = SPAN + LOW

Z1, Z0, Y, X, CORE = 4, 4, 4, 4, 2
Z = Z1 * Z0
DEPTH = ("z1", "z0")
CTX = ("z1", "z0", "y")
HEAD = ("x", "core")

SMEM = pl.BlockSpec(memory_space=pltpu.SMEM)
VMEM = pl.BlockSpec(memory_space=pltpu.VMEM)
ANY = pl.BlockSpec(memory_space=pl.ANY)
HBM = pl.BlockSpec(memory_space=pltpu.HBM)


def dot(a, b, dims, precision=None):
    return lax.dot_general(a, b, ((dims[:1], dims[1:]), ((), ())), precision=precision, preferred_element_type=F32)


def nn(a, b, precision=None):
    return dot(a, b, (1, 0), precision)


def nt(a, b, precision=None):
    return dot(a, b, (1, 1), precision)


def tn(a, b, precision=None):
    return dot(a, b, (0, 0), precision)


def cols(h):
    return slice(h * 256, (h + 1) * 256)


def offsets():
    return lax.broadcasted_iota(jnp.int32, (SPAN, 1), 0).astype(F32)


def decay_mask(rate):
    t = lax.broadcasted_iota(jnp.int32, (SPAN, SPAN), 0)
    s = lax.broadcasted_iota(jnp.int32, (SPAN, SPAN), 1)
    distance = jnp.maximum(t - s, 0).astype(F32)
    return jnp.where(t >= s, jnp.exp(-rate * distance), 0.0)


def joined(spans_ref, towards):
    place = (lax.axis_index("z1") * Z0 + lax.axis_index("z0")) * Y + lax.axis_index("y")
    edges = [place + 1 + j if towards > 0 else place - j for j in range(REACH)]
    cut = [jnp.int32(0)] * REACH
    first = jnp.int32(0)
    for i in range(spans_ref.shape[0] + 1):
        cut = [c + (first == e).astype(jnp.int32) for c, e in zip(cut, edges)]
        if i < spans_ref.shape[0]:
            first = first + spans_ref[i]
    out, total = [], jnp.int32(0)
    for c in cut:
        total = total + c
        out.append(jnp.where(total == 0, 1.0, 0.0).astype(F32))
    return out


def combined(states, links, rate, h):
    total = links[0] * states[0][:, cols(h)].astype(F32)
    for j in range(1, len(states)):
        fade = jnp.exp(jnp.full((1, DV), -rate * (SPAN * j), F32)) * links[j]
        total = total + fade * states[j][:, cols(h)].astype(F32)
    return total


def one_hot(target):
    return jnp.where(lax.broadcasted_iota(jnp.int32, (512, 512), 0) == target, 1.0, 0.0).astype(BF16)


def weight_order():
    row = lax.broadcasted_iota(jnp.int32, (1, 512), 1)
    near = row // 128
    shift = jnp.where(near == 1, NEAR[1], jnp.where(near == 2, NEAR[2], jnp.where(near == 3, NEAR[3], NEAR[0])))
    z = (row // 32) % 4 * Z0 + (lax.axis_index("z0") + shift + Z0) % Z0
    return one_hot((row // 8) % 4 * 128 + (row // 4) % 2 * 64 + z * 4 + row % 4)


def value_order():
    column = lax.broadcasted_iota(jnp.int32, (1, 512), 1)
    return one_hot((column // 4) % 4 * 128 + column // 256 * 64 + (column // 16) % 16 * 4 + column % 4)


def weights_of(q, k, rate):
    return (nt(q, k) * SCALE * decay_mask(rate)).astype(BF16)


def update_kernel(rate_ref, k_hbm, v_hbm, feat_ref, u_ref, own_ref, k_ref, v_ref, sems):
    pairs = ((k_hbm, k_ref), (v_hbm, v_ref), (feat_ref, own_ref))
    copies = [pltpu.make_async_copy(a, b, sems.at[i]) for i, (a, b) in enumerate(pairs)]
    for copy in copies:
        copy.start()
    for copy in copies:
        copy.wait()
    for h in range(HEADS):
        fade = jnp.exp(-rate_ref[h] * (SPAN - offsets()))
        k = k_ref[:, cols(h)].astype(F32) * fade
        u_ref[:, cols(h)] = tn(k, v_ref[:, cols(h)].astype(F32), PREC).astype(BF16)


def near_kernel(s0, s1, s2, s3, a0, out_ref):
    for i, span in enumerate((s0, s1, s2, s3)):
        out_ref[i * SPAN : (i + 1) * SPAN] = span[...]


def second_kernel(rate_ref, spans_ref, own, u1, after_ref, out_ref):
    link = joined(spans_ref, -1)[0]
    for h in range(HEADS):
        out_ref[:, cols(h)] = combined((own, u1), (1.0, link), rate_ref[h], h).astype(BF16)


def forward_kernel(rate_ref, spans_ref, q_ref, k_ref, v_ref, u1, u2, after_ref, normed_ref, state_ref):
    links = joined(spans_ref, -1)
    for h in range(HEADS):
        rate = rate_ref[h]
        q, k, v = q_ref[:, cols(h)], k_ref[:, cols(h)], v_ref[:, cols(h)]
        weights = weights_of(q, k, rate)
        state = combined((u1, u2), links, rate, h)
        state_ref[:, cols(h)] = state.astype(BF16)
        fade = SCALE * jnp.exp(-rate * offsets())
        out = nn(weights, v) + fade * nn(q.astype(F32), state, PREC)
        centred = out - jnp.mean(out, axis=1, keepdims=True)
        rstd = lax.rsqrt(jnp.mean(centred * centred, axis=1, keepdims=True) + EPS)
        normed_ref[:, cols(h)] = centred * rstd
        normed_ref[:, 512 + h * 64 : 576 + h * 64] = jnp.broadcast_to(rstd, (SPAN, 64))


def sort_kernel(w0, w1, w2, w3, out_ref):
    rows = jnp.concatenate([w0[...], w1[...], w2[...], w3[...]], axis=0)
    out_ref[...] = nn(weight_order(), rows).astype(BF16)


def project_kernel(f0, f1, weight_ref, after_ref, out_ref, feat, weight, sems):
    pairs = ((weight_ref, weight), (f0, feat.at[0]), (f1, feat.at[1]))
    copies = [pltpu.make_async_copy(a, b, sems.at[i]) for i, (a, b) in enumerate(pairs)]
    for copy in copies:
        copy.start()
    core = lax.axis_index("core")
    for copy in copies:
        copy.wait()
    for i in range(Y):
        out = jnp.zeros((SPAN, 512), F32)
        for half in range(CORE):
            column = pl.multiple_of(lax.rem(core + half, CORE) * 512, 512)
            out += nt(feat[half, i * SPAN : (i + 1) * SPAN], weight[:, pl.ds(column, 512)])
        high = out.astype(BF16)
        low = (out[:LOW] - high[:LOW].astype(F32)).astype(BF16)
        place = lax.rem(lax.axis_index("y") + i, Y) * X
        for x in range(X):
            out_ref[place + x, :SPAN] = high[:, x * 128 : (x + 1) * 128]
            out_ref[place + x, SPAN:] = low[:, x * 128 : (x + 1) * 128]


def norm_kernel(rate_ref, parts_ref, normed_ref, q_ref, g_ref, source_ref):
    order = value_order()
    sums = []
    for y in range(Y):
        total = parts_ref[y * X].astype(F32)
        for x in range(1, X):
            total = total + parts_ref[y * X + x].astype(F32)
        sums.append(jnp.concatenate([total[:LOW] + total[SPAN:], total[LOW:SPAN]], axis=0))
    whole = jnp.concatenate(sums, axis=1)
    high = whole.astype(BF16)
    low = (whole - high.astype(F32)).astype(BF16)
    norm_grad = nn(high, order) + nn(low, order)
    for h in range(HEADS):
        grad = norm_grad[:, cols(h)]
        normed = normed_ref[:, cols(h)]
        rstd = normed_ref[:, 512 + h * 64 : 513 + h * 64]
        inner = jnp.mean(normed * grad, axis=1, keepdims=True)
        g = rstd * (grad - jnp.mean(grad, axis=1, keepdims=True) - normed * inner)
        g_ref[:, cols(h)] = g.astype(BF16)
        fade = jnp.exp(-rate_ref[h] * offsets())
        source_ref[:, cols(h)] = tn(q_ref[:, cols(h)], (g * fade).astype(BF16)).astype(BF16)


def local_kernel(rate_ref, q_ref, k_ref, v_ref, g_ref, state_ref, qg_ref, kg_ref, vg_ref):
    for h in range(HEADS):
        rate = rate_ref[h]
        q, k, v, g = q_ref[:, cols(h)], k_ref[:, cols(h)], v_ref[:, cols(h)], g_ref[:, cols(h)]
        score = (nt(g, v) * decay_mask(rate)).astype(BF16)
        fade = jnp.exp(-rate * offsets())
        qg = nn(score, k) + fade * nt(g, state_ref[:, cols(h)])
        qg_ref[:, cols(h)] = (SCALE * qg).astype(BF16)
        kg_ref[:, cols(h)] = tn(score, q)
        vg_ref[:, cols(h)] = tn(weights_of(q, k, rate), g)


def final_kernel(rate_ref, spans_ref, s1, s2, s3, k_ref, v_ref, kg_ref, vg_ref, k_out, v_out):
    links = joined(spans_ref, 1)
    for h in range(HEADS):
        rate = rate_ref[h]
        later = combined((s1, s2, s3), links, rate, h).astype(BF16)
        fade = SCALE * jnp.exp(-rate * (SPAN - offsets()))
        k_out[:, cols(h)] = (SCALE * kg_ref[:, cols(h)] + fade * nt(v_ref[:, cols(h)], later)).astype(BF16)
        v_out[:, cols(h)] = (vg_ref[:, cols(h)] + fade * nn(k_ref[:, cols(h)], later)).astype(BF16)


def call(kernel, name, in_specs, outs, flops=0, room=32, **more):
    params = pltpu.CompilerParams(vmem_limit_bytes=room * 1024 * 1024)
    return pl.pallas_call(
        kernel,
        name=name,
        in_specs=in_specs,
        out_shape=outs,
        compiler_params=params,
        cost_estimate=pl.CostEstimate(flops=flops, bytes_accessed=2 << 20, transcendentals=0),
        **more,
    )


def sds(shape, dtype):
    return jax.ShapeDtypeStruct(shape, dtype)


def shift(x, axes, size, by):
    return lax.ppermute(x, axes, [(i, (i + by) % size) for i in range(size)])


def shards(queries, keys, values, out_grad, out_weight, decay_rate, doc_spans):
    block = (SPAN, HEADS * 256)
    split = jnp.broadcast_to(out_weight.reshape(8, X, 1024).transpose(1, 0, 2), (Z1, X, 8, 1024))
    held = lax.all_to_all(split.reshape(Z1 * X, 8, 1024), ("z1", "x"), 0, 0).reshape(128, 1024)
    update, own = call(
        update_kernel,
        "update",
        [SMEM] + [HBM] * 3,
        [sds(block, BF16)] * 2,
        flops=1 << 28,
        scratch_shapes=[pltpu.VMEM(block, BF16), pltpu.VMEM(block, BF16), pltpu.SemaphoreType.DMA((3,))],
    )(decay_rate, *[pltpu.with_memory_space_constraint(x, pltpu.HBM) for x in (keys, values, out_grad)])
    spans = [own] + [shift(own, "y", Y, -j) for j in range(1, Y)]
    u1 = shift(update, CTX, Z * Y, 1)
    second = call(second_kernel, "second", [SMEM, SMEM, VMEM, VMEM, ANY], sds(block, BF16), flops=1 << 20)(
        decay_rate, doc_spans, update, u1, held
    )
    u2 = shift(second, CTX, Z * Y, 2)
    rows = [held] + [shift(held, DEPTH, Z, -s) for s in NEAR[1:]]
    near = call(near_kernel, "near", [VMEM] * 4 + [ANY] * 1, sds((Y * SPAN, 512), BF16))(*spans, held)
    weight = call(sort_kernel, "sort", [VMEM] * 4, sds((512, 1024), BF16), flops=1 << 34)(*rows)
    features = [near, shift(near, "core", CORE, 1)]

    partial = call(
        project_kernel,
        "project",
        [ANY] * 4,
        sds((Y * X, SENT, 128), BF16),
        flops=1 << 30,
        room=32,
        scratch_shapes=[
            pltpu.VMEM((CORE, Y * SPAN, 512), BF16),
            pltpu.VMEM((512, 1024), BF16),
            pltpu.SemaphoreType.DMA((3,)),
        ],
    )(*features, weight, u2)
    normed, state = call(
        forward_kernel,
        "forward",
        [SMEM, SMEM] + [VMEM] * 5 + [ANY],
        [sds((SPAN, 640), F32), sds(block, BF16)],
        flops=1 << 29,
    )(decay_rate, doc_spans, queries, keys, values, u1, u2, partial)
    parts = lax.all_to_all(partial, ("y", "x"), 0, 0)

    g, source = call(norm_kernel, "norm", [SMEM] + [VMEM] * 3, [sds(block, BF16)] * 2, flops=1 << 26)(
        decay_rate, parts, normed, queries
    )
    after = [shift(source, CTX, Z * Y, -j) for j in range(1, REACH + 1)]
    query_grad, kg, vg = call(
        local_kernel, "local", [SMEM] + [VMEM] * 5, [sds(block, BF16), sds(block, F32), sds(block, F32)], flops=1 << 28
    )(decay_rate, queries, keys, values, g, state)
    key_grad, value_grad = call(final_kernel, "final", [SMEM, SMEM] + [VMEM] * 7, [sds(block, BF16)] * 2, flops=1 << 27)(
        decay_rate, doc_spans, *after, keys, values, kg, vg
    )
    return query_grad, key_grad, value_grad


def solution(mesh):
    fine = Mesh(mesh.devices.reshape(Z1, Z0, Y, X, CORE), ("z1", "z0", "y", "x", "core"))
    in_specs = (P(CTX, HEAD), P(CTX, HEAD), P(CTX, HEAD), P(CTX, HEAD), P(HEAD, CTX, None), P(HEAD), P())
    out_specs = (P(CTX, HEAD), P(CTX, HEAD), P(CTX, HEAD))
    return jax.shard_map(shards, mesh=fine, in_specs=in_specs, out_specs=out_specs, check_vma=False)
```

```python
import jax
import jax.numpy as jnp
from jax import lax
from jax.experimental import pallas as pl
from jax.experimental.pallas import tpu as pltpu
from jax.sharding import Mesh, PartitionSpec as P

DK = 256
DV = 256
SPAN = 256
HEADS = 2
REACH = 3
EPS = 1e-05
SCALE = DK**-0.5
F32 = jnp.float32
BF16 = jnp.bfloat16
PREC = lax.Precision.HIGHEST
NEAR = (0, 1, -1, 2)
LOW = 32
SENT = SPAN + LOW

Z1, Z0, Y, X, CORE = 4, 4, 4, 4, 2
Z = Z1 * Z0
DEPTH = ("z1", "z0")
CTX = ("z1", "z0", "y")
HEAD = ("x", "core")

SMEM = pl.BlockSpec(memory_space=pltpu.SMEM)
VMEM = pl.BlockSpec(memory_space=pltpu.VMEM)
ANY = pl.BlockSpec(memory_space=pl.ANY)
HBM = pl.BlockSpec(memory_space=pltpu.HBM)


def dot(a, b, dims, precision=None):
    return lax.dot_general(a, b, ((dims[:1], dims[1:]), ((), ())), precision=precision, preferred_element_type=F32)


def nn(a, b, precision=None):
    return dot(a, b, (1, 0), precision)


def nt(a, b, precision=None):
    return dot(a, b, (1, 1), precision)


def tn(a, b, precision=None):
    return dot(a, b, (0, 0), precision)


def cols(h):
    return slice(h * 256, (h + 1) * 256)


def offsets():
    return lax.broadcasted_iota(jnp.int32, (SPAN, 1), 0).astype(F32)


def decay_mask(rate):
    t = lax.broadcasted_iota(jnp.int32, (SPAN, SPAN), 0)
    s = lax.broadcasted_iota(jnp.int32, (SPAN, SPAN), 1)
    distance = jnp.maximum(t - s, 0).astype(F32)
    return jnp.where(t >= s, jnp.exp(-rate * distance), 0.0)


def joined(spans_ref, towards):
    place = (lax.axis_index("z1") * Z0 + lax.axis_index("z0")) * Y + lax.axis_index("y")
    edges = [place + 1 + j if towards > 0 else place - j for j in range(REACH)]
    cut = [jnp.int32(0)] * REACH
    first = jnp.int32(0)
    for i in range(spans_ref.shape[0] + 1):
        cut = [c + (first == e).astype(jnp.int32) for c, e in zip(cut, edges)]
        if i < spans_ref.shape[0]:
            first = first + spans_ref[i]
    out, total = [], jnp.int32(0)
    for c in cut:
        total = total + c
        out.append(jnp.where(total == 0, 1.0, 0.0).astype(F32))
    return out


def one_hot(target):
    return jnp.where(lax.broadcasted_iota(jnp.int32, (512, 512), 0) == target, 1.0, 0.0).astype(BF16)


def weight_order():
    row = lax.broadcasted_iota(jnp.int32, (1, 512), 1)
    near = row // 128
    shift = jnp.where(near == 1, NEAR[1], jnp.where(near == 2, NEAR[2], jnp.where(near == 3, NEAR[3], NEAR[0])))
    z = (row // 32) % 4 * Z0 + (lax.axis_index("z0") + shift + Z0) % Z0
    return one_hot((row // 8) % 4 * 128 + (row // 4) % 2 * 64 + z * 4 + row % 4)


def value_order():
    column = lax.broadcasted_iota(jnp.int32, (1, 512), 1)
    return one_hot((column // 4) % 4 * 128 + column // 256 * 64 + (column // 16) % 16 * 4 + column % 4)


def weights_of(q, k, rate):
    return (nt(q, k) * SCALE * decay_mask(rate)).astype(BF16)


def scales(aux, h):
    later = [aux[SPAN + 2 * j + h : SPAN + 2 * j + h + 1, :1] for j in range(REACH)]
    return aux[:SPAN, h : h + 1], aux[:SPAN, 2 + h : 3 + h], later


def update_kernel(rate_ref, k_hbm, v_hbm, feat_ref, u_ref, own_ref, k_ref, v_ref, sems):
    pairs = ((k_hbm, k_ref), (v_hbm, v_ref), (feat_ref, own_ref))
    copies = [pltpu.make_async_copy(a, b, sems.at[i]) for i, (a, b) in enumerate(pairs)]
    for copy in copies:
        copy.start()
    for copy in copies:
        copy.wait()
    for h in range(HEADS):
        fade = jnp.exp(-rate_ref[h] * (SPAN - offsets()))
        k, v = k_ref[:, cols(h)].astype(F32) * fade, v_ref[:, cols(h)]
        high = k.astype(BF16)
        low = (k - high.astype(F32)).astype(BF16)
        u_ref[:, cols(h)] = (tn(high, v) + tn(low, v)).astype(BF16)


def split_kernel(w_hbm, out_ref, w_ref, sem):
    copy = pltpu.make_async_copy(w_hbm, w_ref, sem)
    copy.start()
    copy.wait()
    w = w_ref[...].astype(F32)
    rows = jnp.concatenate([w[h] for h in range(HEADS)], axis=0).astype(BF16)
    for z in range(Z1):
        for x in range(X):
            out_ref[z * X + x] = rows[:, x * 1024 : (x + 1) * 1024]


def near_kernel(s0, s1, s3, s2, after_ref, out_ref):
    for i, span in enumerate((s0, s1, s2, s3)):
        out_ref[i * SPAN : (i + 1) * SPAN] = span[...]


def second_kernel(rate_ref, spans_ref, own, u1, after_ref, out_ref, aux_ref):
    before, after = joined(spans_ref, -1), joined(spans_ref, 1)
    lane = lax.broadcasted_iota(jnp.int32, (SPAN, 128), 1)
    rate = jnp.where(lane % 2 == 0, rate_ref[0], rate_ref[1])
    offset = lax.broadcasted_iota(jnp.int32, (SPAN, 128), 0)
    aux_ref[:SPAN] = jnp.exp(-rate * jnp.where(lane < 2, offset, SPAN - offset).astype(F32))
    row = lax.broadcasted_iota(jnp.int32, (8, 128), 0)
    lane = lax.broadcasted_iota(jnp.int32, (8, 128), 1)
    rate = jnp.where(row % 2 == 0, rate_ref[0], rate_ref[1])
    links = [jnp.where(row // 2 == 0, c[0], jnp.where(row // 2 == 1, c[1], c[2])) for c in (before, after)]
    aux_ref[SPAN:] = jnp.exp(-rate * (SPAN * (row // 2)).astype(F32)) * jnp.where(lane == 0, links[1], links[0])
    for h in range(HEADS):
        fade = jnp.exp(jnp.full((1, DV), -rate_ref[h] * SPAN, F32)) * before[0]
        out_ref[:, cols(h)] = (own[:, cols(h)].astype(F32) + fade * u1[:, cols(h)].astype(F32)).astype(BF16)


def forward_kernel(rate_ref, aux, q_ref, k_ref, v_ref, u1, u2, after_ref, normed_ref, state_ref):
    for h in range(HEADS):
        q, k, v = q_ref[:, cols(h)], k_ref[:, cols(h)], v_ref[:, cols(h)]
        weights = weights_of(q, k, rate_ref[h])
        state = aux[SPAN + h : SPAN + h + 1, 1:2] * u1[:, cols(h)].astype(F32)
        state += aux[SPAN + 2 + h : SPAN + 3 + h, 1:2] * u2[:, cols(h)].astype(F32)
        state_ref[:, cols(h)] = state.astype(BF16)
        out = nn(weights, v) + SCALE * scales(aux, h)[0] * nn(q.astype(F32), state, PREC)
        centred = out - jnp.mean(out, axis=1, keepdims=True)
        rstd = lax.rsqrt(jnp.mean(centred * centred, axis=1, keepdims=True) + EPS)
        normed_ref[:, cols(h)] = centred * rstd
        normed_ref[:, 512 + h * 64 : 576 + h * 64] = jnp.broadcast_to(rstd, (SPAN, 64))


def sort_kernel(w0, w1, w2, w3, out_ref):
    rows = jnp.concatenate([w0[...], w1[...], w2[...], w3[...]], axis=0)
    out_ref[...] = nn(weight_order(), rows).astype(BF16)


def project_kernel(f0, f1, weight_ref, out_ref, sums, sems):
    core = lax.axis_index("core")
    copies = []
    for i in range(Y):
        out = jnp.zeros((SPAN, 512), F32)
        for half, feat in enumerate((f0, f1)):
            column = pl.multiple_of(lax.rem(core + half, CORE) * 512, 512)
            out += nt(feat[i * SPAN : (i + 1) * SPAN], weight_ref[:, pl.ds(column, 512)])
        high = out.astype(BF16)
        low = (out[:LOW] - high[:LOW].astype(F32)).astype(BF16)
        for x in range(X):
            sums[i * X + x, :SPAN] = high[:, x * 128 : (x + 1) * 128]
            sums[i * X + x, SPAN:] = low[:, x * 128 : (x + 1) * 128]
        place = lax.rem(lax.axis_index("y") + i, Y) * X
        copies.append(pltpu.make_async_copy(sums.at[pl.ds(i * X, X)], out_ref.at[pl.ds(place, X)], sems.at[i]))
        copies[i].start()
    for copy in copies:
        copy.wait()


def gate_kernel(parts_ref, after_ref, out_ref):
    pass


def norm_kernel(aux, parts_ref, normed_ref, q_ref, g_ref, source_ref):
    order = value_order()
    sums = []
    for y in range(Y):
        total = parts_ref[y * X].astype(F32)
        for x in range(1, X):
            total = total + parts_ref[y * X + x].astype(F32)
        sums.append(jnp.concatenate([total[:LOW] + total[SPAN:], total[LOW:SPAN]], axis=0))
    whole = jnp.concatenate(sums, axis=1)
    high = whole.astype(BF16)
    low = (whole - high.astype(F32)).astype(BF16)
    norm_grad = nn(high, order) + nn(low, order)
    for h in range(HEADS):
        grad = norm_grad[:, cols(h)]
        normed = normed_ref[:, cols(h)]
        rstd = normed_ref[:, 512 + h * 64 : 513 + h * 64]
        inner = jnp.mean(normed * grad, axis=1, keepdims=True)
        g = rstd * (grad - jnp.mean(grad, axis=1, keepdims=True) - normed * inner)
        g_ref[:, cols(h)] = g.astype(BF16)
        source_ref[:, cols(h)] = tn(q_ref[:, cols(h)], (g * scales(aux, h)[0]).astype(BF16)).astype(BF16)


def local_kernel(rate_ref, q_ref, k_ref, v_ref, g_ref, state_ref, qg_ref, kg_ref, vg_ref):
    for h in range(HEADS):
        rate = rate_ref[h]
        q, k, v, g = q_ref[:, cols(h)], k_ref[:, cols(h)], v_ref[:, cols(h)], g_ref[:, cols(h)]
        score = (nt(g, v) * decay_mask(rate)).astype(BF16)
        fade = jnp.exp(-rate * offsets())
        qg = nn(score, k) + fade * nt(g, state_ref[:, cols(h)])
        qg_ref[:, cols(h)] = (SCALE * qg).astype(BF16)
        kg_ref[:, cols(h)] = tn(score, q)
        vg_ref[:, cols(h)] = tn(weights_of(q, k, rate), g)


def final_kernel(aux, s1, s2, s3, k_ref, v_ref, kg_ref, vg_ref, k_out, v_out, k_done, v_done, sems):
    copies = []
    for h in range(HEADS):
        fade, weights = scales(aux, h)[1:]
        later = sum(w * state[:, cols(h)].astype(F32) for w, state in zip(weights, (s1, s2, s3))).astype(BF16)
        fade = SCALE * fade
        k_done[h] = (SCALE * kg_ref[:, cols(h)] + fade * nt(v_ref[:, cols(h)], later)).astype(BF16)
        v_done[h] = (vg_ref[:, cols(h)] + fade * nn(k_ref[:, cols(h)], later)).astype(BF16)
        for i, (done, out) in enumerate(((k_done, k_out), (v_done, v_out))):
            copies.append(pltpu.make_async_copy(done.at[h], out.at[:, pl.ds(h * 256, 256)], sems.at[2 * h + i]))
            copies[-1].start()
    for copy in copies:
        copy.wait()


def call(kernel, name, in_specs, outs, flops=0, room=32, **more):
    params = pltpu.CompilerParams(vmem_limit_bytes=room * 1024 * 1024)
    return pl.pallas_call(
        kernel,
        name=name,
        in_specs=in_specs,
        out_shape=outs,
        compiler_params=params,
        cost_estimate=pl.CostEstimate(flops=flops, bytes_accessed=2 << 20, transcendentals=0),
        **more,
    )


def sds(shape, dtype):
    return jax.ShapeDtypeStruct(shape, dtype)


def shift(x, axes, size, by):
    return lax.ppermute(x, axes, [(i, (i + by) % size) for i in range(size)])


def shards(queries, keys, values, out_grad, out_weight, decay_rate, doc_spans):
    block = (SPAN, HEADS * 256)
    split = call(
        split_kernel,
        "split",
        [HBM],
        sds((Z1 * X, 8, 1024), BF16),
        scratch_shapes=[pltpu.VMEM(out_weight.shape, BF16), pltpu.SemaphoreType.DMA],
    )(pltpu.with_memory_space_constraint(out_weight, pltpu.HBM))
    held = lax.all_to_all(split, ("z1", "x"), 0, 0).reshape(128, 1024)
    update, own = call(
        update_kernel,
        "update",
        [SMEM] + [HBM] * 3,
        [sds(block, BF16)] * 2,
        flops=1 << 28,
        scratch_shapes=[pltpu.VMEM(block, BF16), pltpu.VMEM(block, BF16), pltpu.SemaphoreType.DMA((3,))],
    )(decay_rate, *[pltpu.with_memory_space_constraint(x, pltpu.HBM) for x in (keys, values, out_grad)])
    spans = [own] + [shift(own, "y", Y, -j) for j in range(1, Y)]
    u1 = shift(update, CTX, Z * Y, 1)
    second, aux = call(
        second_kernel,
        "second",
        [SMEM, SMEM, VMEM, VMEM, ANY],
        [sds(block, BF16), sds((SPAN + 8, 128), F32)],
        flops=1 << 20,
    )(decay_rate, doc_spans, update, u1, held)
    u2 = shift(second, CTX, Z * Y, 2)
    rows = [held] + [shift(held, DEPTH, Z, -s) for s in NEAR[1:]]
    weight = call(sort_kernel, "sort", [VMEM] * 4, sds((512, 1024), BF16), flops=1 << 34)(*rows)
    near = call(near_kernel, "near", [VMEM] * 4 + [ANY], sds((Y * SPAN, 512), BF16))(
        spans[0], spans[1], spans[3], spans[2], second
    )
    features = [near, shift(near, "core", CORE, 1)]

    partial = call(
        project_kernel,
        "project",
        [VMEM] * 3,
        sds((Y * X, SENT, 128), BF16),
        flops=1 << 30,
        room=32,
        out_specs=HBM,
        scratch_shapes=[pltpu.VMEM((Y * X, SENT, 128), BF16), pltpu.SemaphoreType.DMA((Y,))],
    )(*features, weight)
    partial = call(
        gate_kernel, "gate", [ANY, ANY], sds((Y * X, SENT, 128), BF16), out_specs=ANY, input_output_aliases={0: 0}
    )(partial, u2)
    normed, state = call(
        forward_kernel,
        "forward",
        [SMEM] + [VMEM] * 6 + [ANY],
        [sds((SPAN, 640), F32), sds(block, BF16)],
        flops=1 << 29,
    )(decay_rate, aux, queries, keys, values, u1, u2, partial)
    parts = lax.all_to_all(partial, ("y", "x"), 0, 0)

    g, source = call(norm_kernel, "norm", [VMEM] * 4, [sds(block, BF16)] * 2, flops=1 << 26)(
        aux, parts, normed, queries
    )
    after = [shift(source, CTX, Z * Y, -j) for j in range(1, REACH + 1)]
    query_grad, kg, vg = call(
        local_kernel, "local", [SMEM] + [VMEM] * 5, [sds(block, BF16), sds(block, F32), sds(block, F32)], flops=1 << 28
    )(decay_rate, queries, keys, values, g, state)
    key_grad, value_grad = call(
        final_kernel,
        "final",
        [VMEM] * 8,
        [sds(block, BF16)] * 2,
        flops=1 << 27,
        out_specs=[HBM, HBM],
        scratch_shapes=[pltpu.VMEM((HEADS, SPAN, 256), BF16)] * 2 + [pltpu.SemaphoreType.DMA((4,))],
    )(aux, *after, keys, values, kg, vg)
    return query_grad, key_grad, value_grad


def solution(mesh):
    fine = Mesh(mesh.devices.reshape(Z1, Z0, Y, X, CORE), ("z1", "z0", "y", "x", "core"))
    in_specs = (P(CTX, HEAD), P(CTX, HEAD), P(CTX, HEAD), P(CTX, HEAD), P(HEAD, CTX, None), P(HEAD), P())
    out_specs = (P(CTX, HEAD), P(CTX, HEAD), P(CTX, HEAD))
    return jax.shard_map(shards, mesh=fine, in_specs=in_specs, out_specs=out_specs, check_vma=False)
```

```python
import jax
import jax.numpy as jnp
from jax import lax
from jax.experimental import pallas as pl
from jax.experimental.pallas import tpu as pltpu
from jax.sharding import Mesh, PartitionSpec as P

DK = 256
DV = 256
SPAN = 256
HEADS = 2
REACH = 3
EPS = 1e-05
SCALE = DK**-0.5
F32 = jnp.float32
BF16 = jnp.bfloat16
PREC = lax.Precision.HIGHEST
NEAR = (0, -1, 1, 2)
LOW = 32
SENT = SPAN + LOW

Z1, Z0, Y, X, CORE = 4, 4, 4, 4, 2
Z = Z1 * Z0
DEPTH = ("z1", "z0")
CTX = ("z1", "z0", "y")
HEAD = ("x", "core")

SMEM = pl.BlockSpec(memory_space=pltpu.SMEM)
VMEM = pl.BlockSpec(memory_space=pltpu.VMEM)
ANY = pl.BlockSpec(memory_space=pl.ANY)
HBM = pl.BlockSpec(memory_space=pltpu.HBM)


def dot(a, b, dims, precision=None):
    return lax.dot_general(a, b, ((dims[:1], dims[1:]), ((), ())), precision=precision, preferred_element_type=F32)


def nn(a, b, precision=None):
    return dot(a, b, (1, 0), precision)


def nt(a, b, precision=None):
    return dot(a, b, (1, 1), precision)


def tn(a, b, precision=None):
    return dot(a, b, (0, 0), precision)


def cols(h):
    return slice(h * 256, (h + 1) * 256)


def offsets():
    return lax.broadcasted_iota(jnp.int32, (SPAN, 1), 0).astype(F32)


def decay_mask(rate):
    t = lax.broadcasted_iota(jnp.int32, (SPAN, SPAN), 0)
    s = lax.broadcasted_iota(jnp.int32, (SPAN, SPAN), 1)
    distance = jnp.maximum(t - s, 0).astype(F32)
    return jnp.where(t >= s, jnp.exp(-rate * distance), 0.0)


def joined(spans_ref, towards):
    place = (lax.axis_index("z1") * Z0 + lax.axis_index("z0")) * Y + lax.axis_index("y")
    edges = [place + 1 + j if towards > 0 else place - j for j in range(REACH)]
    cut = [jnp.int32(0)] * REACH
    first = jnp.int32(0)
    for i in range(spans_ref.shape[0] + 1):
        cut = [c + (first == e).astype(jnp.int32) for c, e in zip(cut, edges)]
        if i < spans_ref.shape[0]:
            first = first + spans_ref[i]
    out, total = [], jnp.int32(0)
    for c in cut:
        total = total + c
        out.append(jnp.where(total == 0, 1.0, 0.0).astype(F32))
    return out


def one_hot(target):
    return jnp.where(lax.broadcasted_iota(jnp.int32, (512, 512), 0) == target, 1.0, 0.0).astype(BF16)


def weight_order():
    row = lax.broadcasted_iota(jnp.int32, (1, 512), 1)
    near = row // 128
    shift = jnp.where(near == 1, NEAR[1], jnp.where(near == 2, NEAR[2], jnp.where(near == 3, NEAR[3], NEAR[0])))
    z = (row // 32) % 4 * Z0 + (lax.axis_index("z0") + shift + Z0) % Z0
    return one_hot((row // 8) % 4 * 128 + (row // 4) % 2 * 64 + z * 4 + row % 4)


def value_order():
    column = lax.broadcasted_iota(jnp.int32, (1, 512), 1)
    return one_hot((column // 4) % 4 * 128 + column // 256 * 64 + (column // 16) % 16 * 4 + column % 4)


def weights_of(q, k, rate):
    return (nt(q, k) * SCALE * decay_mask(rate)).astype(BF16)


def scales(aux, h):
    later = [aux[SPAN + 2 * j + h : SPAN + 2 * j + h + 1, :1] for j in range(REACH)]
    return aux[:SPAN, h : h + 1], aux[:SPAN, 2 + h : 3 + h], later


def update_kernel(rate_ref, k_hbm, v_hbm, feat_ref, u_ref, own_ref, k_ref, v_ref, sems):
    pairs = ((k_hbm, k_ref), (v_hbm, v_ref), (feat_ref, own_ref))
    copies = [pltpu.make_async_copy(a, b, sems.at[i]) for i, (a, b) in enumerate(pairs)]
    for copy in copies:
        copy.start()
    for copy in copies:
        copy.wait()
    for h in range(HEADS):
        fade = jnp.exp(-rate_ref[h] * (SPAN - offsets()))
        k, v = k_ref[:, cols(h)].astype(F32) * fade, v_ref[:, cols(h)]
        high = k.astype(BF16)
        low = (k - high.astype(F32)).astype(BF16)
        u_ref[:, cols(h)] = (tn(high, v) + tn(low, v)).astype(BF16)


def split_kernel(w_hbm, out_ref, w_ref, sem):
    copy = pltpu.make_async_copy(w_hbm, w_ref, sem)
    copy.start()
    copy.wait()
    w = w_ref[...].astype(F32)
    rows = jnp.concatenate([w[h] for h in range(HEADS)], axis=0).astype(BF16)
    for z in range(Z1):
        for x in range(X):
            out_ref[z * X + x] = rows[:, x * 1024 : (x + 1) * 1024]


def near_kernel(s0, s1, s3, s2, after_ref, out_ref):
    for i, span in enumerate((s0, s1, s2, s3)):
        out_ref[i * SPAN : (i + 1) * SPAN] = span[...]


def second_kernel(rate_ref, spans_ref, own, u1, after_ref, out_ref, aux_ref):
    before, after = joined(spans_ref, -1), joined(spans_ref, 1)
    lane = lax.broadcasted_iota(jnp.int32, (SPAN, 128), 1)
    rate = jnp.where(lane % 2 == 0, rate_ref[0], rate_ref[1])
    offset = lax.broadcasted_iota(jnp.int32, (SPAN, 128), 0)
    aux_ref[:SPAN] = jnp.exp(-rate * jnp.where(lane < 2, offset, SPAN - offset).astype(F32))
    row = lax.broadcasted_iota(jnp.int32, (8, 128), 0)
    lane = lax.broadcasted_iota(jnp.int32, (8, 128), 1)
    rate = jnp.where(row % 2 == 0, rate_ref[0], rate_ref[1])
    links = [jnp.where(row // 2 == 0, c[0], jnp.where(row // 2 == 1, c[1], c[2])) for c in (before, after)]
    aux_ref[SPAN:] = jnp.exp(-rate * (SPAN * (row // 2)).astype(F32)) * jnp.where(lane == 0, links[1], links[0])
    for h in range(HEADS):
        fade = jnp.exp(jnp.full((1, DV), -rate_ref[h] * SPAN, F32)) * before[0]
        out_ref[:, cols(h)] = (own[:, cols(h)].astype(F32) + fade * u1[:, cols(h)].astype(F32)).astype(BF16)


def forward_kernel(rate_ref, aux, q_ref, k_ref, v_ref, u1, u2, after_ref, normed_ref, state_ref):
    for h in range(HEADS):
        q, k, v = q_ref[:, cols(h)], k_ref[:, cols(h)], v_ref[:, cols(h)]
        weights = weights_of(q, k, rate_ref[h])
        state = aux[SPAN + h : SPAN + h + 1, 1:2] * u1[:, cols(h)].astype(F32)
        state += aux[SPAN + 2 + h : SPAN + 3 + h, 1:2] * u2[:, cols(h)].astype(F32)
        state_ref[:, cols(h)] = state.astype(BF16)
        out = nn(weights, v) + SCALE * scales(aux, h)[0] * nn(q.astype(F32), state, PREC)
        centred = out - jnp.mean(out, axis=1, keepdims=True)
        rstd = lax.rsqrt(jnp.mean(centred * centred, axis=1, keepdims=True) + EPS)
        normed_ref[:, cols(h)] = centred * rstd
        normed_ref[:, 512 + h * 64 : 576 + h * 64] = jnp.broadcast_to(rstd, (SPAN, 64))


def sort_kernel(w0, w1, w2, w3, out_ref):
    rows = jnp.concatenate([w0[...], w1[...], w2[...], w3[...]], axis=0)
    out_ref[...] = nn(weight_order(), rows).astype(BF16)


def project_kernel(f0, f1, weight_ref, out_ref, sums, sems):
    core = lax.axis_index("core")
    copies = []
    for i in range(Y):
        out = jnp.zeros((SPAN, 512), F32)
        for half, feat in enumerate((f0, f1)):
            column = pl.multiple_of(lax.rem(core + half, CORE) * 512, 512)
            out += nt(feat[i * SPAN : (i + 1) * SPAN], weight_ref[:, pl.ds(column, 512)])
        high = out.astype(BF16)
        low = (out[:LOW] - high[:LOW].astype(F32)).astype(BF16)
        for x in range(X):
            sums[i * X + x, :SPAN] = high[:, x * 128 : (x + 1) * 128]
            sums[i * X + x, SPAN:] = low[:, x * 128 : (x + 1) * 128]
        place = lax.rem(lax.axis_index("y") + i, Y) * X
        copies.append(pltpu.make_async_copy(sums.at[pl.ds(i * X, X)], out_ref.at[pl.ds(place, X)], sems.at[i]))
        copies[i].start()
    for copy in copies:
        copy.wait()


def gate_kernel(parts_ref, after_ref, out_ref):
    pass


def norm_kernel(aux, parts_ref, normed_ref, q_ref, g_ref, source_ref):
    order = value_order()
    sums = []
    for y in range(Y):
        total = parts_ref[y * X].astype(F32)
        for x in range(1, X):
            total = total + parts_ref[y * X + x].astype(F32)
        sums.append(jnp.concatenate([total[:LOW] + total[SPAN:], total[LOW:SPAN]], axis=0))
    whole = jnp.concatenate(sums, axis=1)
    high = whole.astype(BF16)
    low = (whole - high.astype(F32)).astype(BF16)
    norm_grad = nn(high, order) + nn(low, order)
    for h in range(HEADS):
        grad = norm_grad[:, cols(h)]
        normed = normed_ref[:, cols(h)]
        rstd = normed_ref[:, 512 + h * 64 : 513 + h * 64]
        inner = jnp.mean(normed * grad, axis=1, keepdims=True)
        g = rstd * (grad - jnp.mean(grad, axis=1, keepdims=True) - normed * inner)
        g_ref[:, cols(h)] = g.astype(BF16)
        source_ref[:, cols(h)] = tn(q_ref[:, cols(h)], (g * scales(aux, h)[0]).astype(BF16)).astype(BF16)


def local_kernel(rate_ref, q_ref, k_ref, v_ref, g_ref, state_ref, qg_ref, kg_ref, vg_ref):
    for h in range(HEADS):
        rate = rate_ref[h]
        q, k, v, g = q_ref[:, cols(h)], k_ref[:, cols(h)], v_ref[:, cols(h)], g_ref[:, cols(h)]
        score = (nt(g, v) * decay_mask(rate)).astype(BF16)
        fade = jnp.exp(-rate * offsets())
        qg = nn(score, k) + fade * nt(g, state_ref[:, cols(h)])
        qg_ref[:, cols(h)] = (SCALE * qg).astype(BF16)
        kg_ref[:, cols(h)] = tn(score, q)
        vg_ref[:, cols(h)] = tn(weights_of(q, k, rate), g)


def final_kernel(aux, s1, s2, s3, k_ref, v_ref, kg_ref, vg_ref, k_out, v_out, k_done, v_done, sems):
    copies = []
    for h in range(HEADS):
        fade, weights = scales(aux, h)[1:]
        later = sum(w * state[:, cols(h)].astype(F32) for w, state in zip(weights, (s1, s2, s3))).astype(BF16)
        fade = SCALE * fade
        k_done[h] = (SCALE * kg_ref[:, cols(h)] + fade * nt(v_ref[:, cols(h)], later)).astype(BF16)
        v_done[h] = (vg_ref[:, cols(h)] + fade * nn(k_ref[:, cols(h)], later)).astype(BF16)
        for i, (done, out) in enumerate(((k_done, k_out), (v_done, v_out))):
            copies.append(pltpu.make_async_copy(done.at[h], out.at[:, pl.ds(h * 256, 256)], sems.at[2 * h + i]))
            copies[-1].start()
    for copy in copies:
        copy.wait()


def call(kernel, name, in_specs, outs, flops=0, room=32, **more):
    params = pltpu.CompilerParams(vmem_limit_bytes=room * 1024 * 1024)
    return pl.pallas_call(
        kernel,
        name=name,
        in_specs=in_specs,
        out_shape=outs,
        compiler_params=params,
        cost_estimate=pl.CostEstimate(flops=flops, bytes_accessed=2 << 20, transcendentals=0),
        **more,
    )


def sds(shape, dtype):
    return jax.ShapeDtypeStruct(shape, dtype)


def shift(x, axes, size, by):
    return lax.ppermute(x, axes, [(i, (i + by) % size) for i in range(size)])


def shards(queries, keys, values, out_grad, out_weight, decay_rate, doc_spans):
    block = (SPAN, HEADS * 256)
    split = call(
        split_kernel,
        "split",
        [HBM],
        sds((Z1 * X, 8, 1024), BF16),
        scratch_shapes=[pltpu.VMEM(out_weight.shape, BF16), pltpu.SemaphoreType.DMA],
    )(pltpu.with_memory_space_constraint(out_weight, pltpu.HBM))
    held = lax.all_to_all(split, ("z1", "x"), 0, 0).reshape(128, 1024)
    update, own = call(
        update_kernel,
        "update",
        [SMEM] + [HBM] * 3,
        [sds(block, BF16)] * 2,
        flops=1 << 28,
        scratch_shapes=[pltpu.VMEM(block, BF16), pltpu.VMEM(block, BF16), pltpu.SemaphoreType.DMA((3,))],
    )(decay_rate, *[pltpu.with_memory_space_constraint(x, pltpu.HBM) for x in (keys, values, out_grad)])
    spans = [own] + [shift(own, "y", Y, -j) for j in range(1, Y)]
    u1 = shift(update, CTX, Z * Y, 1)
    second, aux = call(
        second_kernel,
        "second",
        [SMEM, SMEM, VMEM, VMEM, ANY],
        [sds(block, BF16), sds((SPAN + 8, 128), F32)],
        flops=1 << 20,
    )(decay_rate, doc_spans, update, u1, held)
    u2 = shift(second, CTX, Z * Y, 2)
    rows = [held] + [shift(held, DEPTH, Z, -s) for s in NEAR[1:]]
    weight = call(sort_kernel, "sort", [VMEM] * 4, sds((512, 1024), BF16), flops=1 << 34)(*rows)
    near = call(near_kernel, "near", [VMEM] * 4 + [ANY], sds((Y * SPAN, 512), BF16))(
        spans[0], spans[1], spans[3], spans[2], second
    )
    features = [near, shift(near, "core", CORE, 1)]

    partial = call(
        project_kernel,
        "project",
        [VMEM] * 3,
        sds((Y * X, SENT, 128), BF16),
        flops=1 << 30,
        room=32,
        out_specs=HBM,
        scratch_shapes=[pltpu.VMEM((Y * X, SENT, 128), BF16), pltpu.SemaphoreType.DMA((Y,))],
    )(*features, weight)
    partial = call(
        gate_kernel, "gate", [ANY, ANY], sds((Y * X, SENT, 128), BF16), out_specs=ANY, input_output_aliases={0: 0}
    )(partial, u2)
    normed, state = call(
        forward_kernel,
        "forward",
        [SMEM] + [VMEM] * 6 + [ANY],
        [sds((SPAN, 640), F32), sds(block, BF16)],
        flops=1 << 29,
    )(decay_rate, aux, queries, keys, values, u1, u2, partial)
    parts = lax.all_to_all(partial, ("y", "x"), 0, 0)

    g, source = call(norm_kernel, "norm", [VMEM] * 4, [sds(block, BF16)] * 2, flops=1 << 26)(
        aux, parts, normed, queries
    )
    after = [shift(source, CTX, Z * Y, -j) for j in range(1, REACH + 1)]
    query_grad, kg, vg = call(
        local_kernel, "local", [SMEM] + [VMEM] * 5, [sds(block, BF16), sds(block, F32), sds(block, F32)], flops=1 << 28
    )(decay_rate, queries, keys, values, g, state)
    key_grad, value_grad = call(
        final_kernel,
        "final",
        [VMEM] * 8,
        [sds(block, BF16)] * 2,
        flops=1 << 27,
        out_specs=[HBM, HBM],
        scratch_shapes=[pltpu.VMEM((HEADS, SPAN, 256), BF16)] * 2 + [pltpu.SemaphoreType.DMA((4,))],
    )(aux, *after, keys, values, kg, vg)
    return query_grad, key_grad, value_grad


def solution(mesh):
    fine = Mesh(mesh.devices.reshape(Z1, Z0, Y, X, CORE), ("z1", "z0", "y", "x", "core"))
    in_specs = (P(CTX, HEAD), P(CTX, HEAD), P(CTX, HEAD), P(CTX, HEAD), P(HEAD, CTX, None), P(HEAD), P())
    out_specs = (P(CTX, HEAD), P(CTX, HEAD), P(CTX, HEAD))
    return jax.shard_map(shards, mesh=fine, in_specs=in_specs, out_specs=out_specs, check_vma=False)
```

```python
import jax
import jax.numpy as jnp
from jax import lax
from jax.experimental import pallas as pl
from jax.experimental.pallas import tpu as pltpu
from jax.sharding import Mesh, PartitionSpec as P

DK = 256
DV = 256
SPAN = 256
HEADS = 2
REACH = 3
EPS = 1e-05
SCALE = DK**-0.5
F32 = jnp.float32
BF16 = jnp.bfloat16
PREC = lax.Precision.HIGHEST
NEAR = (0, -1, 1, 2)
LOW = 32
SENT = SPAN + LOW

Z1, Z0, Y, X, CORE = 4, 4, 4, 4, 2
Z = Z1 * Z0
DEPTH = ("z1", "z0")
CTX = ("z1", "z0", "y")
HEAD = ("x", "core")

SMEM = pl.BlockSpec(memory_space=pltpu.SMEM)
VMEM = pl.BlockSpec(memory_space=pltpu.VMEM)
ANY = pl.BlockSpec(memory_space=pl.ANY)
HBM = pl.BlockSpec(memory_space=pltpu.HBM)


def dot(a, b, dims, precision=None):
    return lax.dot_general(a, b, ((dims[:1], dims[1:]), ((), ())), precision=precision, preferred_element_type=F32)


def nn(a, b, precision=None):
    return dot(a, b, (1, 0), precision)


def nt(a, b, precision=None):
    return dot(a, b, (1, 1), precision)


def tn(a, b, precision=None):
    return dot(a, b, (0, 0), precision)


def cols(h):
    return slice(h * 256, (h + 1) * 256)


def offsets():
    return lax.broadcasted_iota(jnp.int32, (SPAN, 1), 0).astype(F32)


def decay_mask(rate):
    t = lax.broadcasted_iota(jnp.int32, (SPAN, SPAN), 0)
    s = lax.broadcasted_iota(jnp.int32, (SPAN, SPAN), 1)
    distance = jnp.maximum(t - s, 0).astype(F32)
    return jnp.where(t >= s, jnp.exp(-rate * distance), 0.0)


def joined(spans_ref, towards):
    place = (lax.axis_index("z1") * Z0 + lax.axis_index("z0")) * Y + lax.axis_index("y")
    edges = [place + 1 + j if towards > 0 else place - j for j in range(REACH)]
    cut = [jnp.int32(0)] * REACH
    first = jnp.int32(0)
    for i in range(spans_ref.shape[0] + 1):
        cut = [c + (first == e).astype(jnp.int32) for c, e in zip(cut, edges)]
        if i < spans_ref.shape[0]:
            first = first + spans_ref[i]
    out, total = [], jnp.int32(0)
    for c in cut:
        total = total + c
        out.append(jnp.where(total == 0, 1.0, 0.0).astype(F32))
    return out


def one_hot(target):
    return jnp.where(lax.broadcasted_iota(jnp.int32, (512, 512), 0) == target, 1.0, 0.0).astype(BF16)


def weight_order():
    row = lax.broadcasted_iota(jnp.int32, (1, 512), 1)
    near = row // 128
    shift = jnp.where(near == 1, NEAR[1], jnp.where(near == 2, NEAR[2], jnp.where(near == 3, NEAR[3], NEAR[0])))
    z = (row // 32) % 4 * Z0 + (lax.axis_index("z0") + shift + Z0) % Z0
    return one_hot((row // 8) % 4 * 128 + (row // 4) % 2 * 64 + z * 4 + row % 4)


def value_order():
    column = lax.broadcasted_iota(jnp.int32, (1, 512), 1)
    return one_hot((column // 4) % 4 * 128 + column // 256 * 64 + (column // 16) % 16 * 4 + column % 4)


def weights_of(q, k, rate):
    return (nt(q, k) * SCALE * decay_mask(rate)).astype(BF16)


def scales(aux, h):
    later = [aux[SPAN + 2 * j + h : SPAN + 2 * j + h + 1, :1] for j in range(REACH)]
    return aux[:SPAN, h : h + 1], aux[:SPAN, 2 + h : 3 + h], later


def update_kernel(rate_ref, k_ref, v_ref, u_ref):
    for h in range(HEADS):
        fade = jnp.exp(-rate_ref[:, h : h + 1] * (SPAN - offsets()))
        k, v = k_ref[:, cols(h)].astype(F32) * fade, v_ref[:, cols(h)]
        high = k.astype(BF16)
        low = (k - high.astype(F32)).astype(BF16)
        u_ref[:, cols(h)] = (tn(high, v) + tn(low, v)).astype(BF16)


def split_kernel(w_hbm, rate_hbm, k_hbm, v_hbm, feat_hbm, out_ref, rate_ref, k_ref, v_ref, own_ref, w_ref, sems):
    pairs = ((w_hbm, w_ref), (rate_hbm, rate_ref), (k_hbm, k_ref), (v_hbm, v_ref), (feat_hbm, own_ref))
    copies = [pltpu.make_async_copy(a, b, sems.at[i]) for i, (a, b) in enumerate(pairs)]
    for copy in copies:
        copy.start()
    copies[0].wait()
    w = w_ref[...].astype(F32)
    rows = jnp.concatenate([w[h] for h in range(HEADS)], axis=0).astype(BF16)
    for z in range(Z1):
        for x in range(X):
            out_ref[z * X + x] = rows[:, x * 1024 : (x + 1) * 1024]
    for copy in copies[1:]:
        copy.wait()


def near_kernel(s0, s3, s1, s2, after_ref, out_ref):
    for i, span in enumerate((s0, s1, s2, s3)):
        out_ref[i * SPAN : (i + 1) * SPAN] = span[...]


def second_kernel(rate_ref, spans_ref, own, u1, after_ref, out_ref, aux_ref):
    before, after = joined(spans_ref, -1), joined(spans_ref, 1)
    lane = lax.broadcasted_iota(jnp.int32, (SPAN, 128), 1)
    rate = jnp.where(lane % 2 == 0, rate_ref[0], rate_ref[1])
    offset = lax.broadcasted_iota(jnp.int32, (SPAN, 128), 0)
    aux_ref[:SPAN] = jnp.exp(-rate * jnp.where(lane < 2, offset, SPAN - offset).astype(F32))
    row = lax.broadcasted_iota(jnp.int32, (8, 128), 0)
    lane = lax.broadcasted_iota(jnp.int32, (8, 128), 1)
    rate = jnp.where(row % 2 == 0, rate_ref[0], rate_ref[1])
    links = [jnp.where(row // 2 == 0, c[0], jnp.where(row // 2 == 1, c[1], c[2])) for c in (before, after)]
    aux_ref[SPAN:] = jnp.exp(-rate * (SPAN * (row // 2)).astype(F32)) * jnp.where(lane == 0, links[1], links[0])
    for h in range(HEADS):
        fade = jnp.exp(jnp.full((1, DV), -rate_ref[h] * SPAN, F32)) * before[0]
        out_ref[:, cols(h)] = (own[:, cols(h)].astype(F32) + fade * u1[:, cols(h)].astype(F32)).astype(BF16)


def forward_kernel(rate_ref, aux, q_ref, k_ref, v_ref, u1, u2, after_ref, normed_ref, state_ref):
    for h in range(HEADS):
        q, k, v = q_ref[:, cols(h)], k_ref[:, cols(h)], v_ref[:, cols(h)]
        weights = weights_of(q, k, rate_ref[h])
        state = aux[SPAN + h : SPAN + h + 1, 1:2] * u1[:, cols(h)].astype(F32)
        state += aux[SPAN + 2 + h : SPAN + 3 + h, 1:2] * u2[:, cols(h)].astype(F32)
        state_ref[:, cols(h)] = state.astype(BF16)
        out = nn(weights, v) + SCALE * scales(aux, h)[0] * nn(q.astype(F32), state, PREC)
        centred = out - jnp.mean(out, axis=1, keepdims=True)
        rstd = lax.rsqrt(jnp.mean(centred * centred, axis=1, keepdims=True) + EPS)
        normed_ref[:, cols(h)] = centred * rstd
        normed_ref[:, 512 + h * 64 : 576 + h * 64] = jnp.broadcast_to(rstd, (SPAN, 64))


def sort_kernel(w0, w1, w2, w3, out_ref):
    rows = jnp.concatenate([w0[...], w1[...], w2[...], w3[...]], axis=0)
    out_ref[...] = nn(weight_order(), rows).astype(BF16)


def project_kernel(f0, f1, weight_ref, out_ref, sums, sems):
    core = lax.axis_index("core")
    copies = []
    for i in range(Y):
        out = jnp.zeros((SPAN, 512), F32)
        for half, feat in enumerate((f0, f1)):
            column = pl.multiple_of(lax.rem(core + half, CORE) * 512, 512)
            out += nt(feat[i * SPAN : (i + 1) * SPAN], weight_ref[:, pl.ds(column, 512)])
        high = out.astype(BF16)
        low = (out[:LOW] - high[:LOW].astype(F32)).astype(BF16)
        for x in range(X):
            sums[i * X + x, :SPAN] = high[:, x * 128 : (x + 1) * 128]
            sums[i * X + x, SPAN:] = low[:, x * 128 : (x + 1) * 128]
        place = lax.rem(lax.axis_index("y") + i, Y) * X
        copies.append(pltpu.make_async_copy(sums.at[pl.ds(i * X, X)], out_ref.at[pl.ds(place, X)], sems.at[i]))
        copies[i].start()
    for copy in copies:
        copy.wait()


def gate_kernel(parts_ref, after_ref, out_ref):
    pass


def norm_kernel(aux, parts_ref, normed_ref, q_ref, g_ref, source_ref):
    order = value_order()
    sums = []
    for y in range(Y):
        total = parts_ref[y * X].astype(F32)
        for x in range(1, X):
            total = total + parts_ref[y * X + x].astype(F32)
        sums.append(jnp.concatenate([total[:LOW] + total[SPAN:], total[LOW:SPAN]], axis=0))
    whole = jnp.concatenate(sums, axis=1)
    high = whole.astype(BF16)
    low = (whole - high.astype(F32)).astype(BF16)
    norm_grad = nn(high, order) + nn(low, order)
    for h in range(HEADS):
        grad = norm_grad[:, cols(h)]
        normed = normed_ref[:, cols(h)]
        rstd = normed_ref[:, 512 + h * 64 : 513 + h * 64]
        inner = jnp.mean(normed * grad, axis=1, keepdims=True)
        g = rstd * (grad - jnp.mean(grad, axis=1, keepdims=True) - normed * inner)
        g_ref[:, cols(h)] = g.astype(BF16)
        source_ref[:, cols(h)] = tn(q_ref[:, cols(h)], (g * scales(aux, h)[0]).astype(BF16)).astype(BF16)


def local_kernel(rate_ref, q_ref, k_ref, v_ref, g_ref, state_ref, qg_ref, kg_ref, vg_ref):
    for h in range(HEADS):
        rate = rate_ref[h]
        q, k, v, g = q_ref[:, cols(h)], k_ref[:, cols(h)], v_ref[:, cols(h)], g_ref[:, cols(h)]
        score = (nt(g, v) * decay_mask(rate)).astype(BF16)
        fade = jnp.exp(-rate * offsets())
        qg = nn(score, k) + fade * nt(g, state_ref[:, cols(h)])
        qg_ref[:, cols(h)] = (SCALE * qg).astype(BF16)
        kg_ref[:, cols(h)] = tn(score, q)
        vg_ref[:, cols(h)] = tn(weights_of(q, k, rate), g)


def final_kernel(aux, s1, s2, s3, k_ref, v_ref, kg_ref, vg_ref, k_out, v_out, k_done, v_done, sems):
    copies = []
    for h in range(HEADS):
        fade, weights = scales(aux, h)[1:]
        later = sum(w * state[:, cols(h)].astype(F32) for w, state in zip(weights, (s1, s2, s3))).astype(BF16)
        fade = SCALE * fade
        k_done[h] = (SCALE * kg_ref[:, cols(h)] + fade * nt(v_ref[:, cols(h)], later)).astype(BF16)
        v_done[h] = (vg_ref[:, cols(h)] + fade * nn(k_ref[:, cols(h)], later)).astype(BF16)
        for i, (done, out) in enumerate(((k_done, k_out), (v_done, v_out))):
            copies.append(pltpu.make_async_copy(done.at[h], out.at[:, pl.ds(h * 256, 256)], sems.at[2 * h + i]))
            copies[-1].start()
    for copy in copies:
        copy.wait()


def call(kernel, name, in_specs, outs, flops=0, room=32, **more):
    params = pltpu.CompilerParams(vmem_limit_bytes=room * 1024 * 1024)
    return pl.pallas_call(
        kernel,
        name=name,
        in_specs=in_specs,
        out_shape=outs,
        compiler_params=params,
        cost_estimate=pl.CostEstimate(flops=flops, bytes_accessed=2 << 20, transcendentals=0),
        **more,
    )


def sds(shape, dtype):
    return jax.ShapeDtypeStruct(shape, dtype)


def shift(x, axes, size, by):
    return lax.ppermute(x, axes, [(i, (i + by) % size) for i in range(size)])


def shards(queries, keys, values, out_grad, out_weight, decay_rate, doc_spans):
    block = (SPAN, HEADS * 256)
    arrays = (out_weight, decay_rate.reshape(1, HEADS), keys, values, out_grad)
    split, rate, k_near, v_near, own = call(
        split_kernel,
        "split",
        [HBM] * 5,
        [sds((Z1 * X, 8, 1024), BF16), sds((1, HEADS), F32)] + [sds(block, BF16)] * 3,
        scratch_shapes=[pltpu.VMEM(out_weight.shape, BF16), pltpu.SemaphoreType.DMA((5,))],
    )(*[pltpu.with_memory_space_constraint(x, pltpu.HBM) for x in arrays])
    held = lax.all_to_all(split, ("z1", "x"), 0, 0).reshape(128, 1024)
    update = call(update_kernel, "update", [VMEM] * 3, sds(block, BF16), flops=1 << 28)(rate, k_near, v_near)
    spans = [own] + [shift(own, "y", Y, -j) for j in range(1, Y)]
    u1 = shift(update, CTX, Z * Y, 1)
    second, aux = call(
        second_kernel,
        "second",
        [SMEM, SMEM, VMEM, VMEM, ANY],
        [sds(block, BF16), sds((SPAN + 8, 128), F32)],
        flops=1 << 20,
    )(decay_rate, doc_spans, update, u1, held)
    u2 = shift(second, CTX, Z * Y, 2)
    rows = [held] + [shift(held, DEPTH, Z, -s) for s in NEAR[1:]]
    weight = call(sort_kernel, "sort", [VMEM] * 4, sds((512, 1024), BF16), flops=1 << 34)(*rows)
    near = call(near_kernel, "near", [VMEM] * 4 + [ANY], sds((Y * SPAN, 512), BF16))(
        spans[0], spans[3], spans[1], spans[2], second
    )
    features = [near, shift(near, "core", CORE, 1)]

    partial = call(
        project_kernel,
        "project",
        [VMEM] * 3,
        sds((Y * X, SENT, 128), BF16),
        flops=1 << 30,
        room=32,
        out_specs=HBM,
        scratch_shapes=[pltpu.VMEM((Y * X, SENT, 128), BF16), pltpu.SemaphoreType.DMA((Y,))],
    )(*features, weight)
    partial = call(
        gate_kernel, "gate", [ANY, ANY], sds((Y * X, SENT, 128), BF16), out_specs=ANY, input_output_aliases={0: 0}
    )(partial, u2)
    normed, state = call(
        forward_kernel,
        "forward",
        [SMEM] + [VMEM] * 6 + [ANY],
        [sds((SPAN, 640), F32), sds(block, BF16)],
        flops=1 << 29,
    )(decay_rate, aux, queries, keys, values, u1, u2, partial)
    parts = lax.all_to_all(partial, ("y", "x"), 0, 0)

    g, source = call(norm_kernel, "norm", [VMEM] * 4, [sds(block, BF16)] * 2, flops=1 << 26)(
        aux, parts, normed, queries
    )
    after = [shift(source, CTX, Z * Y, -j) for j in range(1, REACH + 1)]
    query_grad, kg, vg = call(
        local_kernel, "local", [SMEM] + [VMEM] * 5, [sds(block, BF16), sds(block, F32), sds(block, F32)], flops=1 << 28
    )(decay_rate, queries, keys, values, g, state)
    key_grad, value_grad = call(
        final_kernel,
        "final",
        [VMEM] * 8,
        [sds(block, BF16)] * 2,
        flops=1 << 27,
        out_specs=[HBM, HBM],
        scratch_shapes=[pltpu.VMEM((HEADS, SPAN, 256), BF16)] * 2 + [pltpu.SemaphoreType.DMA((4,))],
    )(aux, *after, keys, values, kg, vg)
    return query_grad, key_grad, value_grad


def solution(mesh):
    fine = Mesh(mesh.devices.reshape(Z1, Z0, Y, X, CORE), ("z1", "z0", "y", "x", "core"))
    in_specs = (P(CTX, HEAD), P(CTX, HEAD), P(CTX, HEAD), P(CTX, HEAD), P(HEAD, CTX, None), P(HEAD), P())
    out_specs = (P(CTX, HEAD), P(CTX, HEAD), P(CTX, HEAD))
    return jax.shard_map(shards, mesh=fine, in_specs=in_specs, out_specs=out_specs, check_vma=False)
```
